32 devices in a mesh: grp: 2 (over core), pts: 16 (over z, y, x).
Axes of the slice: x: 2, y: 2, z: 4, core: 2. Of those that a mesh axis runs over, the one named last changes fastest.
Arguments:
- element_attribute_table: bfloat16 [262144, 512], P(('grp', 'pts')), parts along dimension 0, may hold values from -6 to 6
- active_group_tally: int32 [32], P(('grp', 'pts')), parts along dimension 0, may hold values from 48 to 64, as said below
- group_destination_part: int32 [2048], P(('grp', 'pts')), parts along dimension 0, may hold values from 0 to 15, as said below
- element_vertex_permutation: int32 [2048, 128], P(('grp', 'pts')), parts along dimension 0, may hold values from 0 to 127, each once within a row
- softness_factor: float32 [8], replicated, may hold values from 0.15 to 0.6
- entry_projection_coefficients: bfloat16 [512, 1024], replicated, may hold values from -0.25 to 0.25
- partition_score_coefficients: bfloat16 [8, 64, 256], replicated, may hold values from -0.75 to 0.75
- summary_query_key_coefficients: bfloat16 [64, 192], replicated, may hold values from -0.75 to 0.75
- final_projection_coefficients: bfloat16 [512, 512], replicated, may hold values from -0.25 to 0.25
Outputs:
- point_features: bfloat16 [262144, 512], P(('grp', 'pts')), parts along dimension 0
The draws below stay inside these ranges and needn't reach their ends.
There are 2 independent parts, one for each index of `grp`. The reference program is written for one: setup_inputs(seed, part) draws one part's arguments, and reference() takes and returns one part's arrays. A program takes and returns all parts, laid end to end along the dimension named above; an argument that names none is the same for every part. Nothing has to cross between parts.
Inputs may be any that keep to these rules, and one draw needn't show every extreme that they name: The live blocks of a device are its first active_group_tally slots; some device has all 64 live. `group_destination_part`: no device names a point shard in more than 4 of its slots; some point shard is named exactly 4 times by the live blocks of every device. `element_vertex_permutation`: each row is a permutation.
All inputs are finite; a program needn't handle non-finite values.
Results may differ from the reference program's by a relative error of at most 0.0016.
Values may be sent and summed in bfloat16 or wider, within the bound.
No kernel may reach another device: no remote copies, remote signals or barrier semaphores. Data moves between devices by JAX's collectives and lax.ppermute only.
A program may use at most 192 MiB of HBM per device.

```python
import math
import jax
import jax.numpy as jnp
from jax import lax

C = 512
ATTENDER_AMOUNT = 8
S = 256
BLOCK = 128
BLK_DEV = 64
HD = 64
CAP = 4
NB = 1024
NCELL = 131072
N_PTS = 16


def draw_active_group_tally(key, part):
    least = BLK_DEV - BLK_DEV // 4
    counts = jax.random.randint(jax.random.fold_in(key, 21), (N_PTS,), least, BLK_DEV + 1)
    fullest = jax.random.randint(jax.random.fold_in(key, 22), (), 0, N_PTS)
    return jnp.where(jnp.arange(N_PTS) == fullest, BLK_DEV, counts).astype(jnp.int32)


def draw_group_destination_part(key, part):
    least = BLK_DEV - BLK_DEV // 4
    others_total = (N_PTS - 1) * CAP
    target = jax.random.randint(jax.random.fold_in(key, 11), (), 0, N_PTS)

    def one_device(device_key):
        first_key, second_key = jax.random.split(device_key)
        others = jnp.arange(others_total, dtype=jnp.int32) // CAP
        others = others + (others >= target).astype(jnp.int32)
        others = others[jax.random.permutation(first_key, others_total)]
        other_scores = 2 * jnp.arange(others_total, dtype=jnp.int32) + 1
        places = jax.random.permutation(second_key, least - CAP + 1)[:CAP].astype(jnp.int32)
        target_scores = 2 * places
        values = jnp.concatenate([others, jnp.full((CAP,), target, jnp.int32)])
        scores = jnp.concatenate([other_scores, target_scores])
        order = jnp.argsort(scores, stable=True)
        return values[order][:BLK_DEV]
    device_keys = jax.random.split(jax.random.fold_in(key, 12), N_PTS)
    return jax.vmap(one_device)(device_keys).reshape(-1).astype(jnp.int32)


def strengthened(entries, own_key, source, target, blocks, factor):
    owner, partner = [(jnp.arange(entries.shape[position]) // (entries.shape[position] // blocks)).reshape([-1 if axis == position else 1 for axis in range(entries.ndim)]) for position in (source, target)]
    chosen = jax.random.permutation(own_key, blocks)[partner]
    strong = (owner == chosen) | (owner == (partner + blocks // 2) % blocks)
    return jnp.where(strong, factor * entries, entries)


def steps_of(rng, shape, cuts, smallest, largest):
    level = 1.0
    for axis_at, blocks in cuts:
        draws = jax.random.uniform(jax.random.fold_in(jax.random.fold_in(rng, 6), axis_at), (blocks,), jnp.float32, smallest / len(cuts), largest / len(cuts))
        level = level * jnp.repeat(jnp.exp(draws), shape[axis_at] // blocks).reshape((-1,) + (1,) * (len(shape) - 1 - axis_at))
    return level


def scatter_about(stream_key, extent, deviation, most, cuts=(), kind=jnp.bfloat16):
    array = deviation * jax.random.normal(stream_key, extent, jnp.float32)
    if cuts:
        array = array * steps_of(stream_key, extent, cuts, -0.22, 0.18)
    return jnp.clip(array, -most, most).astype(kind)


def bell_draw_with(own_key, extent, scale, reach, cuts, heavy, kind=jnp.bfloat16):
    result = scale * jax.random.normal(own_key, extent, jnp.float32)
    if cuts:
        result = result * steps_of(own_key, extent, cuts, -0.22, 0.18)
    return jnp.clip(strengthened(result, jax.random.fold_in(own_key, 3), *heavy), -reach, reach).astype(kind)


def setup_inputs(seed: int = 0, part: int = 0) -> dict:
    key_of = jax.random.split(jax.random.key(seed), 10)
    part_splits = jax.random.split(jax.random.fold_in(key_of[9], part), 10)
    return {
        "element_attribute_table": bell_draw_with(part_splits[0], (NCELL, C), 1.0, 6.0, ((0, 16),), (0, 1, 16, 2.0)),
        "active_group_tally": draw_active_group_tally(jax.random.fold_in(jax.random.fold_in(key_of[9], part), 71), part),
        "group_destination_part": draw_group_destination_part(jax.random.fold_in(jax.random.fold_in(key_of[9], part), 71), part),
        "element_vertex_permutation": jax.vmap(lambda own: jax.random.permutation(own, BLOCK))(jax.random.split(part_splits[3], NB)).reshape((NB, BLOCK)).astype(jnp.int32),
        "softness_factor": jnp.clip(jnp.exp(jax.random.uniform(key_of[4], (ATTENDER_AMOUNT,), jnp.float32, math.log(0.15), math.log(0.6))), 0.15, 0.6),
        "entry_projection_coefficients": scatter_about(key_of[5], (C, 2 * C), C ** -0.5, 0.25),
        "partition_score_coefficients": scatter_about(key_of[6], (ATTENDER_AMOUNT, HD, S), HD ** -0.5, 0.75),
        "summary_query_key_coefficients": scatter_about(key_of[7], (HD, 3 * HD), HD ** -0.5, 0.75),
        "final_projection_coefficients": scatter_about(key_of[8], (C, C), C ** -0.5, 0.25),
    }


NORM_EPS = 1e-05
SLICE_EPS = 1e-05

def normalize_rows(point_rows):
    values = point_rows.astype(jnp.float32)
    centre = lax.optimization_barrier(jnp.mean(values, axis=-1, keepdims=True))
    spread = lax.optimization_barrier(jnp.mean(jnp.square(values - centre), axis=-1, keepdims=True))
    return ((values - centre) * lax.rsqrt(spread + NORM_EPS)).astype(jnp.bfloat16)

def slice_attention(tokens, summary_query_key_coefficients):
    head_width = tokens.shape[-1]
    project = jnp.einsum('hsd,de->hse', tokens, summary_query_key_coefficients.astype(jnp.float32), precision=lax.Precision.HIGHEST)
    queries = project[..., :head_width]
    slice_keys = project[..., head_width:2 * head_width]
    slice_values = project[..., 2 * head_width:]
    scores = jnp.einsum('hsd,htd->hst', queries, slice_keys, precision=lax.Precision.HIGHEST) * head_width ** (-0.5)
    powered_entries = jnp.exp(scores)
    attend = powered_entries / lax.optimization_barrier(jnp.sum(powered_entries, axis=-1, keepdims=True))
    return jnp.einsum('hst,htd->hsd', attend, slice_values, precision=lax.Precision.HIGHEST).astype(jnp.bfloat16)

def reference(element_attribute_table, active_group_tally, group_destination_part, element_vertex_permutation, softness_factor, entry_projection_coefficients, partition_score_coefficients, summary_query_key_coefficients, final_projection_coefficients):
    block_total = N_PTS * BLK_DEV
    blocks = jnp.take_along_axis(element_attribute_table.reshape(block_total, BLOCK, C), element_vertex_permutation[:, :, None].astype(jnp.int32), axis=1)
    positions = jnp.arange(BLK_DEV, dtype=jnp.int32)
    block_live = positions[None, :] < active_group_tally[:, None]
    device_rows = blocks.reshape(N_PTS, BLK_DEV * BLOCK, C)
    row_live = jnp.repeat(block_live.astype(jnp.float32), BLOCK, axis=1)

    def slice_weights(point_rows):
        mixed = jnp.dot(normalize_rows(point_rows), entry_projection_coefficients, preferred_element_type=jnp.float32)
        feature_matrix = mixed[:, :C].astype(jnp.bfloat16)
        middle_result = mixed[:, C:].astype(jnp.bfloat16)
        partition_raw_scores = jnp.einsum('rhd,hds->rhs', middle_result.reshape(-1, ATTENDER_AMOUNT, HD).astype(jnp.float32), partition_score_coefficients.astype(jnp.float32))
        partition_raw_scores = partition_raw_scores / softness_factor[None, :, None]
        powered_entries = jnp.exp(partition_raw_scores)
        weights = (powered_entries / lax.optimization_barrier(jnp.sum(powered_entries, axis=-1, keepdims=True))).astype(jnp.bfloat16)
        return (feature_matrix, weights)

    def accumulate(carry, item):
        point_rows, live_mask = item
        feature_matrix, weights = slice_weights(point_rows)
        masked = weights * live_mask[:, None, None].astype(jnp.bfloat16)
        numer = jnp.einsum('rhs,rhd->hsd', masked.astype(jnp.float32), feature_matrix.reshape(-1, ATTENDER_AMOUNT, HD).astype(jnp.float32))
        denom = lax.optimization_barrier(jnp.sum(masked.astype(jnp.float32), axis=0))
        return ((carry[0] + numer, carry[1] + denom), None)
    start = (jnp.zeros((ATTENDER_AMOUNT, S, HD), jnp.float32), jnp.zeros((ATTENDER_AMOUNT, S), jnp.float32))
    (numer, denom), _ = lax.scan(accumulate, start, (device_rows, row_live))
    tokens = numer / (denom[..., None] + SLICE_EPS)
    mixed_tokens = slice_attention(tokens, summary_query_key_coefficients)

    def finish(item):
        point_rows, live_mask = item
        feature_matrix, weights = slice_weights(point_rows)
        spread_back = jnp.einsum('rhs,hsd->rhd', weights.astype(jnp.float32), mixed_tokens.astype(jnp.float32))
        spread_back = spread_back.astype(jnp.bfloat16).reshape(-1, C)
        update = jnp.dot(spread_back, final_projection_coefficients, preferred_element_type=jnp.float32)
        return ((point_rows.astype(jnp.float32) + update) * live_mask[:, None]).astype(jnp.bfloat16)
    results = lax.map(finish, (device_rows, row_live))
    block_results = results.reshape(block_total, BLOCK, C)
    dest_table = group_destination_part.reshape(N_PTS, BLK_DEV).astype(jnp.int32)
    earlier = (dest_table[:, :, None] == dest_table[:, None, :]) & (positions[None, None, :] < positions[None, :, None])
    rank = lax.optimization_barrier(jnp.sum(earlier.astype(jnp.int32), axis=2))
    owners = jnp.arange(N_PTS, dtype=jnp.int32)[:, None]
    target = dest_table * (N_PTS * CAP) + owners * CAP + rank
    dummy = N_PTS * N_PTS * CAP
    target = jnp.where(block_live, target, dummy).reshape(-1).astype(jnp.int32)
    placed = jnp.zeros((dummy + 1, BLOCK, C), jnp.bfloat16).at[target].set(block_results)
    return placed[:dummy].reshape(-1, C)
```

```python
import functools
import math

import jax
import jax.numpy as jnp
from jax import lax
from jax.experimental import pallas as pl
from jax.experimental.pallas import tpu as pltpu
from jax.sharding import PartitionSpec as P

NORM_EPS = 1e-05
SLICE_EPS = 1e-05
LOG2E = math.log2(math.e)
MIB = 1 << 20
ANY = pl.BlockSpec(memory_space=pl.ANY)
SMEM = pl.BlockSpec(memory_space=pltpu.SMEM)
VMEM = pl.BlockSpec(memory_space=pltpu.VMEM)
HIDDEN = pl.CostEstimate(flops=0, bytes_accessed=0, transcendentals=0)


def dot(a, b, contract, precision=None):
    return lax.dot_general(
        a, b, (contract, ((), ())), preferred_element_type=jnp.float32, precision=precision
    )


def normalize_rows(point_rows):
    values = point_rows.astype(jnp.float32)
    centre = jnp.mean(values, axis=-1, keepdims=True)
    values = values - centre
    spread = jnp.mean(jnp.square(values), axis=-1, keepdims=True)
    return (values * lax.rsqrt(spread + NORM_EPS)).astype(jnp.bfloat16)


def passing(carried, first_input, first_output):
    shapes = [pltpu.HBM(a.shape, a.dtype) for a in carried]
    aliases = {first_input + i: first_output + i for i in range(len(carried))}
    return [ANY] * len(carried), shapes, aliases


def gather_kernel(passed, count, per_peer, rows, pick_ref, perm_ref, table_ref, *refs):
    refs = refs[passed:]
    outs = refs[:count]
    taken, made, in_sem, out_sem = refs[count:]

    def fetch(j, q):
        return pltpu.make_async_copy(
            table_ref.at[pick_ref[j * per_peer + q]], taken.at[j, q], in_sem.at[j, q]
        )

    def store(j):
        return pltpu.make_async_copy(made.at[j], outs[j], out_sem.at[j])

    for j in range(count):

        @pl.loop(0, per_peer)
        def _(q):
            fetch(j, q).start()

    for j in range(count):

        @pl.loop(0, per_peer)
        def _(q):
            fetch(j, q).wait()
            wanted = perm_ref[pl.ds(pick_ref[j * per_peer + q], 1), :]
            level = lax.broadcasted_iota(jnp.int32, (rows, rows), 0)
            picking = jnp.where(level == wanted, 1.0, 0.0).astype(jnp.bfloat16)
            made[j, pl.ds(pl.multiple_of(q * rows, rows), rows), :] = dot(
                picking, taken[j, q], ((0,), (0,))
            ).astype(jnp.bfloat16)

        store(j).start()
    for j in range(count):
        store(j).wait()


def gather_blocks(pick, perm, table, per_peer, carried=()):
    count = pick.shape[0] // per_peer
    blocks, rows = perm.shape
    channels = table.shape[-1]
    size = count * per_peer * rows * channels
    specs, shapes, aliases = passing(carried, 3, 0)
    out = pl.pallas_call(
        functools.partial(gather_kernel, 2 * len(carried), count, per_peer, rows),
        out_shape=shapes
        + [pltpu.HBM((per_peer * rows, channels), jnp.bfloat16)] * count,
        in_specs=[SMEM, VMEM, ANY] + specs,
        out_specs=specs + [ANY] * count,
        input_output_aliases=aliases,
        scratch_shapes=[
            pltpu.VMEM((count, per_peer, rows, channels), jnp.bfloat16),
            pltpu.VMEM((count, per_peer * rows, channels), jnp.bfloat16),
            pltpu.SemaphoreType.DMA((count, per_peer)),
            pltpu.SemaphoreType.DMA((count,)),
        ],
        compiler_params=pltpu.CompilerParams(vmem_limit_bytes=48 * MIB),
        cost_estimate=HIDDEN,
        name="gather_blocks",
    )(pick, perm, table.reshape(blocks, rows, channels), *carried)
    return out[len(carried) :], out[: len(carried)]


def slice_powers(raw_scores, factor):
    scaled = raw_scores * factor
    return jnp.exp2(scaled - jnp.max(scaled, axis=0, keepdims=True))


def head_scores(middle, score_ref):
    heads, _, width = score_ref.shape
    made = [dot(score_ref[h], middle[h * width : (h + 1) * width], ((1,), (0,))) for h in range(1)]
    for h in range(heads):
        if h + 1 < heads:
            made.append(
                dot(score_ref[h + 1], middle[(h + 1) * width : (h + 2) * width], ((1,), (0,)))
            )
        yield h, made[h]


def summary_kernel(
    passed, start, live_ref, count_ref, factor_ref, before_ref, rows_ref, entry_ref, score_ref, *refs
):
    out_ref, total = refs[passed], refs[-1]
    heads, slices, width = score_ref.shape
    tile = rows_ref.shape[0]
    step = pl.program_id(0)
    channels = heads * width
    height = total.shape[1]

    @pl.when(step == 0)
    def _():
        total[...] = before_ref[...] if start else jnp.zeros_like(total)

    left = live_ref[0] - (step + start) * tile

    @pl.when(left > 0)
    def _():
        normed = normalize_rows(rows_ref[...])
        middle = dot(entry_ref[channels:, :], normed, ((1,), (1,))).astype(jnp.bfloat16)
        features = dot(entry_ref[:channels, :], normed, ((1,), (1,)))
        alive = lax.broadcasted_iota(jnp.int32, (1, tile), 1) < left
        for h, scores in head_scores(middle, score_ref):
            span = slice(h * width, (h + 1) * width)
            powers = slice_powers(scores, factor_ref[h])
            share = jnp.where(alive, 1.0 / jnp.sum(powers, axis=0, keepdims=True), 0.0)
            terms = jnp.concatenate(
                [features[span] * share, jnp.broadcast_to(share, (height - width, tile))], axis=0
            ).astype(jnp.bfloat16)
            total[h] += dot(terms, powers.astype(jnp.bfloat16), ((1,), (1,)))

    @pl.when(step == pl.num_programs(0) - 1)
    def _():
        if out_ref.shape == total.shape:
            out_ref[...] = total[...]
        else:
            pieces, _, piece = out_ref.shape
            per_head = slices // piece
            level = lax.broadcasted_iota(jnp.int32, (height, piece), 0)
            for p in range(pieces):
                at = p % per_head * piece
                part = total[p // per_head, :, at : at + piece]
                sent = count_ref[p].astype(jnp.float32)
                out_ref[p] = jnp.where(level == width + 1, sent, part).astype(out_ref.dtype)


def summarize(
    live_rows, counts, factors, before, table, entry_t, score_t, steps, carried=(), tile=1024
):
    heads, slices, width = score_t.shape
    pieces = counts.shape[0]
    total_rows, channels = table.shape
    tile = total_rows // steps[2]
    sums = jax.ShapeDtypeStruct((heads, width + 16, slices), jnp.float32)
    shape = sums
    if steps[1] == steps[2]:
        shape = jax.ShapeDtypeStruct(
            (pieces, width + 16, heads * slices // pieces), jnp.bfloat16
        )
    specs, shapes, aliases = passing(carried, 7, 0)
    out = pl.pallas_call(
        functools.partial(summary_kernel, 2 * len(carried), steps[0]),
        grid=(steps[1] - steps[0],),
        out_shape=shapes + [shape],
        in_specs=[
            SMEM,
            SMEM,
            SMEM,
            pl.BlockSpec(before.shape, lambda i: (0,) * before.ndim),
            pl.BlockSpec((tile, channels), lambda i: (i + steps[0], 0)),
            pl.BlockSpec(entry_t.shape, lambda i: (0, 0)),
            pl.BlockSpec(score_t.shape, lambda i: (0, 0, 0)),
        ]
        + specs,
        out_specs=specs + [pl.BlockSpec(shape.shape, lambda i: (0, 0, 0))],
        scratch_shapes=[pltpu.VMEM(sums.shape, jnp.float32)],
        input_output_aliases=aliases,
        compiler_params=pltpu.CompilerParams(vmem_limit_bytes=40 * MIB),
        cost_estimate=HIDDEN,
        name="summarize",
    )(live_rows, counts, factors, before, table, entry_t, score_t, *carried)
    return out[-1], out[:-1]


def tokens_kernel(passed, partials_ref, *refs):
    out_ref = refs[passed]
    pieces, width, piece = out_ref.shape
    sums = partials_ref[0].astype(jnp.float32)
    for p in range(1, pieces):
        sums += partials_ref[p].astype(jnp.float32)
    tokens = (sums[:width] / (sums[width : width + 1] + SLICE_EPS)).astype(out_ref.dtype)
    for p in range(pieces):
        out_ref[p] = tokens


def own_tokens(partials, width, carried=()):
    pieces, _, piece = partials.shape
    specs, shapes, aliases = passing(carried, 1, 0)
    out = pl.pallas_call(
        functools.partial(tokens_kernel, 2 * len(carried)),
        out_shape=shapes + [jax.ShapeDtypeStruct((pieces, width, piece), jnp.bfloat16)],
        in_specs=[VMEM] + specs,
        out_specs=specs + [VMEM],
        input_output_aliases=aliases,
        compiler_params=pltpu.CompilerParams(vmem_limit_bytes=16 * MIB),
        cost_estimate=HIDDEN,
        name="own_tokens",
    )(partials, *carried)
    return out[-1], out[:-1]


def attend_kernel(passed, tokens_ref, maps_ref, *refs):
    out_ref = refs[passed]
    heads, width, slices = out_ref.shape
    per_head = tokens_ref.shape[0] // heads
    exact = lax.Precision.HIGHEST
    maps = maps_ref[...].astype(jnp.float32)
    for h in range(heads):
        tokens = jnp.concatenate(
            [tokens_ref[h * per_head + i].astype(jnp.float32) for i in range(per_head)], axis=1
        )
        project = dot(maps, tokens, ((1,), (0,)), exact)
        queries, keys, values = (project[i * width : (i + 1) * width] for i in range(3))
        scores = dot(keys, queries, ((0,), (0,)), exact) * width**-0.5
        powers = jnp.exp(scores - jnp.max(scores, axis=0, keepdims=True))
        mixed = dot(values, powers, ((1,), (0,)), exact)
        out_ref[h] = (mixed / jnp.sum(powers, axis=0, keepdims=True)).astype(jnp.bfloat16)


def attend(tokens, maps_t, heads, carried=()):
    pieces, width, piece = tokens.shape
    specs, shapes, aliases = passing(carried, 2, 0)
    out = pl.pallas_call(
        functools.partial(attend_kernel, 2 * len(carried)),
        out_shape=shapes + [jax.ShapeDtypeStruct((heads, width, pieces // heads * piece), jnp.bfloat16)],
        in_specs=[VMEM, VMEM] + specs,
        out_specs=specs + [VMEM],
        input_output_aliases=aliases,
        compiler_params=pltpu.CompilerParams(vmem_limit_bytes=48 * MIB),
        cost_estimate=HIDDEN,
        name="attend",
    )(tokens, maps_t, *carried)
    return out[-1], out[:-1]


def entry_of(ids, chunk):
    rank = ids[0]
    for i, other in enumerate(ids[1:]):
        rank = jnp.where(chunk == i + 1, other, rank)
    return rank


def finish_kernel(ids, block_rows, extra, place_ref, valid_ref, factor_ref, *refs):
    chunks = len(ids)
    xs = refs[:chunks]
    entry_ref, score_ref, mixed_ref, final_ref = refs[chunks : chunks + 4]
    out_ref, held = refs[chunks + 4 + extra], refs[-1]
    heads, slices, width = score_ref.shape
    tile = held.shape[0]
    chunk, step = pl.program_id(0), pl.program_id(1)
    for i in range(chunks):

        @pl.when(chunk == i)
        def _():
            held[...] = xs[i][...]

    left = valid_ref[place_ref[entry_of(ids, chunk)]] * block_rows - step * tile

    @pl.when(left <= 0)
    def _():
        out_ref[...] = jnp.zeros_like(out_ref)

    @pl.when(left > 0)
    def _():
        rows = held[...]
        normed = normalize_rows(rows)
        middle = dot(entry_ref[...], normed, ((1,), (1,))).astype(jnp.bfloat16)
        spread = []
        for h, scores in head_scores(middle, score_ref):
            powers = slice_powers(scores, factor_ref[h])
            share = 1.0 / jnp.sum(powers, axis=0, keepdims=True)
            back = dot(mixed_ref[h], powers.astype(jnp.bfloat16), ((1,), (0,)))
            spread.append((back * share).astype(jnp.bfloat16))
        spread = jnp.concatenate(spread, axis=0)
        update = dot(spread, final_ref[...], ((0,), (0,)))
        done = rows.astype(jnp.float32) + update
        alive = lax.broadcasted_iota(jnp.int32, (tile, 1), 0) < left
        out_ref[...] = jnp.where(alive, done, 0.0).astype(out_ref.dtype)


def finish(
    ids, block_rows, place, valid, factors, xs, entry_t, score_t, mixed, final, out, total_rows, carried=(), tile=512
):
    heads, slices, width = score_t.shape
    chunk_rows, channels = xs[0].shape
    tile = min(tile, chunk_rows)
    tiles = chunk_rows // tile
    chunks = len(xs)

    def chunk_spec(i):
        def index(j, t, *_):
            return jnp.where(j == i, t, jnp.where(j < i, 0, tiles - 1)), 0

        return pl.BlockSpec((tile, channels), index)

    def whole(a):
        return pl.BlockSpec(a.shape, lambda *_: (0,) * a.ndim)

    kept = list(carried) + ([] if out is None else [out])
    specs, shapes, aliases = passing(kept, 3 + chunks + 4, 0)
    if out is None:
        shapes = shapes + [jax.ShapeDtypeStruct((total_rows, channels), jnp.bfloat16)]
    out_specs = [ANY] * (len(shapes) - 1) + [
        pl.BlockSpec((tile, channels), lambda j, t, place, *_: (place[entry_of(ids, j)] * tiles + t, 0))
    ]
    work = chunks * chunk_rows
    result = pl.pallas_call(
        functools.partial(finish_kernel, ids, block_rows, len(kept) + len(shapes) - 1),
        out_shape=shapes,
        grid_spec=pltpu.PrefetchScalarGridSpec(
            num_scalar_prefetch=3,
            grid=(chunks, tiles),
            in_specs=[chunk_spec(i) for i in range(chunks)]
            + [whole(entry_t), whole(score_t), whole(mixed), whole(final)]
            + specs,
            out_specs=out_specs,
            scratch_shapes=[pltpu.VMEM((tile, channels), jnp.bfloat16)],
        ),
        input_output_aliases=aliases,
        compiler_params=pltpu.CompilerParams(vmem_limit_bytes=48 * MIB),
        cost_estimate=HIDDEN,
        name="finish",
    )(place, valid, factors, *xs, entry_t, score_t, mixed, final, *kept)
    return result[-1], result[:-1]


def per_device(
    element_attribute_table,
    active_group_tally,
    group_destination_part,
    element_vertex_permutation,
    softness_factor,
    entry_projection_coefficients,
    partition_score_coefficients,
    summary_query_key_coefficients,
    final_projection_coefficients,
):
    block_count, block_rows = element_vertex_permutation.shape
    total_rows, channels = element_attribute_table.shape
    heads, width, slices = partition_score_coefficients.shape
    shards = lax.axis_size("pts")
    here = lax.axis_index("pts")
    per_peer = max(1, (block_count + shards - 1) // shards)
    chunk_rows = per_peer * block_rows

    paired = shards & (shards - 1) == 0

    def target(k):
        return here ^ k if paired else (here + k) % shards

    def source(k):
        return here ^ k if paired else (here - k) % shards

    def send(chunk, k):
        pairs = [(i, i ^ k if paired else (i + k) % shards) for i in range(shards)]
        return lax.ppermute(chunk, "pts", pairs)

    far = list(range(shards // 2, shards))
    near = list(range(1, shards // 2))
    waves = [far[:1] + near[:1], far[1:2], far[2:3], far[3:4], far[4:5], far[5:7] + near[1:3]]
    far, near = far[7:], near[3:]
    while far or near:
        waves.append(far[:1] + near[: 1 if far else 2])
        far, near = far[1:], near[1 if far else 2 :]
    ranks = [k for wave in waves for k in wave] + [0]

    positions = jnp.arange(block_count, dtype=jnp.int32)
    live = positions < active_group_tally[0]
    earlier = (group_destination_part[:, None] == group_destination_part[None, :]) & (
        positions[None, :] < positions[:, None]
    )
    rank = jnp.sum(earlier.astype(jnp.int32), axis=1)
    slot = jnp.where(live, group_destination_part * per_peer + rank, -1)
    targets = jnp.stack([target(k) for k in ranks])
    wanted = (targets[:, None] * per_peer + jnp.arange(per_peer, dtype=jnp.int32)).reshape(-1)
    pick = jnp.sum(jnp.where(wanted[:, None] == slot[None, :], positions[None, :], 0), axis=1)
    shard_ids = jnp.arange(shards, dtype=jnp.int32)
    counts = jnp.sum(
        (live[None, :] & (group_destination_part[None, :] == shard_ids[:, None])).astype(jnp.int32),
        axis=1,
    )
    factors = LOG2E / softness_factor
    entry_t = entry_projection_coefficients.T
    score_t = partition_score_coefficients.transpose(0, 2, 1)
    maps_t = summary_query_key_coefficients.T

    arrived = {}
    held = {}
    order = jnp.zeros((8, 128), jnp.int32)

    def gather(offsets, order):
        at = ranks.index(offsets[0]) * per_peer
        chunks, (order,) = gather_blocks(
            pick[at : at + len(offsets) * per_peer],
            element_vertex_permutation,
            element_attribute_table,
            per_peer,
            (order,),
        )
        held.update(zip(offsets, chunks))
        return order

    def depart(wave):
        for k in wave:
            arrived[k] = send(held.pop(k), k)

    def carry(order):
        return (order,) + tuple(held.values())

    def release(carried, wave):
        held.update(zip(list(held), carried[1:]))
        depart(wave)
        return carried[0]

    order = gather(waves[0], order)
    depart(waves[0])
    order = gather(waves[1] + waves[2] + waves[3], order)
    depart(waves[1])
    live_rows = active_group_tally * block_rows
    weights = (element_attribute_table, entry_t, score_t)
    steps = 8
    begun, carried = summarize(
        live_rows, counts, factors, jnp.zeros((8, 128)), *weights, (0, steps - 1, steps), carry(order)
    )
    order = release(carried, waves[2])
    early = waves[0] + waves[1]
    partial, carried = summarize(
        live_rows,
        counts,
        factors,
        begun,
        *weights,
        (steps - 1, steps, steps),
        carry(order) + tuple(arrived[k] for k in early),
    )
    arrived.update(zip(early, carried[-len(early) :]))
    order = release(carried[: -len(early)], waves[3])
    partials = lax.all_to_all(partial, "pts", 0, 0, tiled=True)
    order = gather([k for wave in waves[4:] for k in wave] + [0], order)
    arrived[0] = held.pop(0)
    received = partials[:, width + 1, 0].astype(jnp.int32)
    tokens, carried = own_tokens(partials, width, carry(order))
    order = release(carried, waves[4])
    tokens = lax.all_to_all(tokens, "pts", 0, 0, tiled=True)
    mixed, carried = attend(tokens, maps_t, heads, carry(order))
    order = release(carried, waves[5])

    middle_t = entry_t[channels:]
    sources = jnp.stack([source(k) for k in ranks])
    groups = [[0] + waves[0] + waves[1] + waves[2], waves[3], waves[4], waves[5][::2], waves[5][1::2]]
    groups += waves[6:]
    out = None
    for i, group in enumerate(groups):
        if not group:
            continue
        out, carried = finish(
            [ranks.index(k) for k in group],
            block_rows,
            sources,
            received,
            factors,
            [arrived[k] for k in group],
            middle_t,
            score_t,
            mixed,
            final_projection_coefficients,
            out,
            shards * chunk_rows,
            carry(order),
        )
        order = release(carried, waves[6 + i] if 6 + i < len(waves) else [])
    return out


def solution(mesh):
    placed = (
        P(("grp", "pts"), None),
        P(("grp", "pts")),
        P(("grp", "pts")),
        P(("grp", "pts"), None),
        P(),
        P(),
        P(),
        P(),
        P(),
    )
    return jax.shard_map(
        per_device, mesh=mesh, in_specs=placed, out_specs=P(("grp", "pts"), None), check_vma=False
    )
```

```python
import functools
import math

import jax
import jax.numpy as jnp
from jax import lax
from jax.experimental import pallas as pl
from jax.experimental.pallas import tpu as pltpu
from jax.sharding import PartitionSpec as P

NORM_EPS = 1e-05
SLICE_EPS = 1e-05
LOG2E = math.log2(math.e)
MIB = 1 << 20
EXACT = lax.Precision.HIGHEST
ANY = pl.BlockSpec(memory_space=pl.ANY)
SMEM = pl.BlockSpec(memory_space=pltpu.SMEM)
VMEM = pl.BlockSpec(memory_space=pltpu.VMEM)
HIDDEN = pl.CostEstimate(flops=0, bytes_accessed=0, transcendentals=0)


def dot(a, b, contract, precision=None):
    return lax.dot_general(
        a, b, (contract, ((), ())), preferred_element_type=jnp.float32, precision=precision
    )


def normalize_rows(point_rows):
    values = point_rows.astype(jnp.float32)
    centre = jnp.mean(values, axis=-1, keepdims=True)
    values = values - centre
    spread = jnp.mean(jnp.square(values), axis=-1, keepdims=True)
    return (values * lax.rsqrt(spread + NORM_EPS)).astype(jnp.bfloat16)


def passing(carried, first_input, first_output):
    shapes = [pltpu.HBM(a.shape, a.dtype) for a in carried]
    aliases = {first_input + i: first_output + i for i in range(len(carried))}
    return [ANY] * len(carried), shapes, aliases


def plan_slots(per_peer, tally_ref, part_ref, slots_ref, counts_ref):
    shards = counts_ref.shape[0]

    @pl.loop(0, shards)
    def _(p):
        counts_ref[p] = 0
        for q in range(per_peer):
            slots_ref[p * per_peer + q] = 0

    @pl.loop(0, tally_ref[0])
    def _(b):
        part = part_ref[b]
        at = counts_ref[part]
        slots_ref[part * per_peer + jnp.minimum(at, per_peer - 1)] = b
        counts_ref[part] = at + 1


def gather_kernel(plan, offsets, per_peer, rows, here_ref, *refs):
    count = len(offsets)
    *refs, taken, made, in_sem, out_sem = refs
    outs = refs[-count:]
    if plan:
        tally_ref, part_ref, perm_ref, table_ref, slots_ref, counts_ref = refs[:6]
        plan_slots(per_peer, tally_ref, part_ref, slots_ref, counts_ref)
    else:
        slots_ref, perm_ref, table_ref = refs[:3]

    def block(j, q):
        return slots_ref[(here_ref[0] ^ offsets[j]) * per_peer + q]

    def fetch(j, q):
        return pltpu.make_async_copy(
            table_ref.at[block(j, q)], taken.at[j, q], in_sem.at[j, q]
        )

    def store(j):
        return pltpu.make_async_copy(made.at[j], outs[j], out_sem.at[j])

    for j in range(count):

        @pl.loop(0, per_peer)
        def _(q):
            fetch(j, q).start()

    for j in range(count):

        @pl.loop(0, per_peer)
        def _(q):
            fetch(j, q).wait()
            wanted = perm_ref[pl.ds(block(j, q), 1), :]
            level = lax.broadcasted_iota(jnp.int32, (rows, rows), 0)
            picking = jnp.where(level == wanted, 1.0, 0.0).astype(jnp.bfloat16)
            made[j, pl.ds(pl.multiple_of(q * rows, rows), rows), :] = dot(
                picking, taken[j, q], ((0,), (0,))
            ).astype(jnp.bfloat16)

        store(j).start()
    for j in range(count):
        store(j).wait()


def gather_blocks(here, slots, perm, table, offsets, per_peer, carried=(), shards=0):
    count = len(offsets)
    blocks, rows = perm.shape
    channels = table.shape[-1]
    plan = len(slots) > 1
    specs, shapes, aliases = passing(carried, 3 + len(slots), 0)
    planned = [
        jax.ShapeDtypeStruct((shards * per_peer,), jnp.int32),
        jax.ShapeDtypeStruct((shards,), jnp.int32),
    ] * plan
    out = pl.pallas_call(
        functools.partial(gather_kernel, plan, offsets, per_peer, rows),
        out_shape=shapes + planned + [pltpu.HBM((per_peer * rows, channels), jnp.bfloat16)] * count,
        in_specs=[SMEM] * (1 + len(slots)) + [VMEM, ANY] + specs,
        out_specs=specs + [SMEM] * len(planned) + [ANY] * count,
        input_output_aliases=aliases,
        scratch_shapes=[
            pltpu.VMEM((count, per_peer, rows, channels), jnp.bfloat16),
            pltpu.VMEM((count, per_peer * rows, channels), jnp.bfloat16),
            pltpu.SemaphoreType.DMA((count, per_peer)),
            pltpu.SemaphoreType.DMA((count,)),
        ],
        compiler_params=pltpu.CompilerParams(vmem_limit_bytes=48 * MIB),
        cost_estimate=HIDDEN,
        name="gather_blocks",
    )(here, *slots, perm, table.reshape(blocks, rows, channels), *carried)
    return out[len(carried) :], out[: len(carried)]


def slice_powers(raw_scores, factor):
    scaled = raw_scores * factor
    return jnp.exp2(scaled - jnp.max(scaled, axis=0, keepdims=True))


def head_scores(middle, score_ref):
    heads, _, width = score_ref.shape
    made = [dot(score_ref[h], middle[h * width : (h + 1) * width], ((1,), (0,))) for h in range(1)]
    for h in range(heads):
        if h + 1 < heads:
            made.append(
                dot(score_ref[h + 1], middle[(h + 1) * width : (h + 2) * width], ((1,), (0,)))
            )
        yield h, made[h]


def summary_kernel(
    pieces, start, passed, seat_ref, live_ref, factor_ref, before_ref, tail_ref, rows_ref, entry_ref, score_ref, *refs
):
    out_refs, total = refs[passed : passed + pieces], refs[-1]
    heads, slices, width = score_ref.shape
    tile = rows_ref.shape[0]
    step = pl.program_id(0)
    channels = heads * width
    height = total.shape[1]

    @pl.when(step == 0)
    def _():
        total[...] = before_ref[...] if start else jnp.zeros_like(total)

    left = live_ref[0] - (start + step) * tile

    @pl.when(left > 0)
    def _():
        normed = normalize_rows(rows_ref[...])
        middle = dot(entry_ref[channels:, :], normed, ((1,), (1,))).astype(jnp.bfloat16)
        features = dot(entry_ref[:channels, :], normed, ((1,), (1,)))
        alive = lax.broadcasted_iota(jnp.int32, (1, tile), 1) < left
        for h, scores in head_scores(middle, score_ref):
            span = slice(h * width, (h + 1) * width)
            powers = slice_powers(scores, factor_ref[h])
            share = jnp.where(alive, 1.0 / jnp.sum(powers, axis=0, keepdims=True), 0.0)
            terms = jnp.concatenate(
                [features[span] * share, jnp.broadcast_to(share, (height - width, tile))], axis=0
            ).astype(jnp.bfloat16)
            total[h] += dot(terms, powers.astype(jnp.bfloat16), ((1,), (1,)))

    @pl.when(step == pl.num_programs(0) - 1)
    def _():
        if not pieces:
            refs[passed][...] = total[...]
        share = heads // max(pieces, 1)
        level = lax.broadcasted_iota(jnp.int32, (height - width, slices), 0)
        for p in range(pieces):
            for i in range(share):
                part = total[(seat_ref[0] ^ p) * share + i]
                rest = jnp.where(level == 0, part[width:], tail_ref[...])
                out_refs[p][i, :width] = part[:width].astype(jnp.bfloat16)
                out_refs[p][i, width:] = rest.astype(jnp.bfloat16)


def summarize(
    seat, live_rows, factors, before, tail, table, entry_t, score_t, steps, pieces, carried=()
):
    heads, slices, width = score_t.shape
    total_rows, channels = table.shape
    tile = total_rows // steps[2]
    whole = jax.ShapeDtypeStruct((heads, width + tail.shape[0], slices), jnp.float32)
    specs, shapes, aliases = passing(carried, 8, 0)
    outs = [jax.ShapeDtypeStruct((heads // max(pieces, 1),) + whole.shape[1:], jnp.bfloat16)]
    outs = outs * pieces or [whole]
    out = pl.pallas_call(
        functools.partial(summary_kernel, pieces, steps[0], 2 * len(carried)),
        grid=(steps[1] - steps[0],),
        out_shape=shapes + outs,
        in_specs=[
            SMEM,
            SMEM,
            SMEM,
            pl.BlockSpec(before.shape, lambda i: (0,) * before.ndim),
            pl.BlockSpec(tail.shape, lambda i: (0, 0)),
            pl.BlockSpec((tile, channels), lambda i: (steps[0] + i, 0)),
            pl.BlockSpec(entry_t.shape, lambda i: (0, 0)),
            pl.BlockSpec(score_t.shape, lambda i: (0, 0, 0)),
        ]
        + specs,
        out_specs=specs + [pl.BlockSpec(o.shape, lambda i: (0, 0, 0)) for o in outs],
        scratch_shapes=[pltpu.VMEM(whole.shape, jnp.float32)],
        input_output_aliases=aliases,
        compiler_params=pltpu.CompilerParams(vmem_limit_bytes=40 * MIB),
        cost_estimate=HIDDEN,
        name="summarize",
    )(
        seat,
        live_rows,
        factors,
        before,
        tail,
        pltpu.with_memory_space_constraint(table, pltpu.HBM),
        entry_t,
        score_t,
        *carried,
    )
    return out[len(carried) :], out[: len(carried)]


def small_call(kernel, name, inputs, shapes, carried, scalars=0, **kwargs):
    specs, passed, aliases = passing(carried, len(inputs), 0)
    out = pl.pallas_call(
        functools.partial(kernel, **kwargs),
        out_shape=passed + shapes,
        in_specs=[SMEM] * scalars + [VMEM] * (len(inputs) - scalars) + specs,
        out_specs=specs + [VMEM] * len(shapes),
        input_output_aliases=aliases,
        compiler_params=pltpu.CompilerParams(vmem_limit_bytes=16 * MIB),
        cost_estimate=HIDDEN,
        name=name,
    )(*inputs, *carried)
    return out[len(carried) :], out[: len(carried)]


def total_of(refs, *at):
    total = refs[0][at].astype(jnp.float32)
    for ref in refs[1:]:
        total += ref[at].astype(jnp.float32)
    return total


def add_kernel(*refs, parts):
    refs[-1][...] = total_of(refs[:parts], Ellipsis).astype(refs[-1].dtype)


def attend_kernel(*refs, parts):
    maps_ref, sums, out_ref, tail_ref = refs[0], refs[1 : 1 + parts], refs[-2], refs[-1]
    heads, width, slices = out_ref.shape
    maps = maps_ref[...].astype(jnp.float32)
    for h in range(heads):
        total = total_of(sums, h)
        tokens = total[:width] / (total[width : width + 1] + SLICE_EPS)
        project = dot(maps, tokens, ((1,), (0,)), EXACT)
        queries, keys, values = (project[i * width : (i + 1) * width] for i in range(3))
        scores = dot(keys, queries, ((0,), (0,)), EXACT) * width**-0.5
        powers = jnp.exp(scores - jnp.max(scores, axis=0, keepdims=True))
        mixed = dot(values, powers, ((1,), (0,)), EXACT)
        out_ref[h] = (mixed / jnp.sum(powers, axis=0, keepdims=True)).astype(jnp.bfloat16)
        if h == 0:
            tail_ref[...] = total[width:]


def join_kernel(seat_ref, *refs, parts):
    out_ref = refs[-1]
    share = refs[0].shape[0]
    for p in range(parts):
        out_ref[pl.ds((seat_ref[0] ^ p) * share, share)] = refs[p][...]


def entry_of(ids, chunk):
    rank = ids[0]
    for i, other in enumerate(ids[1:]):
        rank = jnp.where(chunk == i + 1, other, rank)
    return rank


def finish_kernel(ids, block_rows, extra, place_ref, valid_ref, factor_ref, *refs):
    chunks = len(ids)
    xs = refs[:chunks]
    entry_ref, score_ref, mixed_ref, final_ref = refs[chunks : chunks + 4]
    out_ref, held = refs[chunks + 4 + extra], refs[-1]
    heads, slices, width = score_ref.shape
    tile = held.shape[0]
    chunk, step = pl.program_id(0), pl.program_id(1)
    for i in range(chunks):

        @pl.when(chunk == i)
        def _():
            held[...] = xs[i][...]

    left = valid_ref[place_ref[entry_of(ids, chunk)]] * block_rows - step * tile

    @pl.when(left <= 0)
    def _():
        out_ref[...] = jnp.zeros_like(out_ref)

    @pl.when(left > 0)
    def _():
        rows = held[...]
        normed = normalize_rows(rows)
        middle = dot(entry_ref[...], normed, ((1,), (1,))).astype(jnp.bfloat16)
        spread = []
        for h, scores in head_scores(middle, score_ref):
            powers = slice_powers(scores, factor_ref[h])
            share = 1.0 / jnp.sum(powers, axis=0, keepdims=True)
            back = dot(mixed_ref[h], powers.astype(jnp.bfloat16), ((1,), (0,)))
            spread.append((back * share).astype(jnp.bfloat16))
        spread = jnp.concatenate(spread, axis=0)
        update = dot(spread, final_ref[...], ((0,), (0,)))
        done = rows.astype(jnp.float32) + update
        alive = lax.broadcasted_iota(jnp.int32, (tile, 1), 0) < left
        out_ref[...] = jnp.where(alive, done, 0.0).astype(out_ref.dtype)


def finish(
    ids, block_rows, place, valid, factors, xs, entry_t, score_t, mixed, final, out, total_rows, carried=(), tile=512
):
    heads, slices, width = score_t.shape
    chunk_rows, channels = xs[0].shape
    tile = min(tile, chunk_rows)
    tiles = chunk_rows // tile
    chunks = len(xs)

    def chunk_spec(i):
        def index(j, t, *_):
            return jnp.where(j == i, t, jnp.where(j < i, 0, tiles - 1)), 0

        return pl.BlockSpec((tile, channels), index)

    def whole(a):
        return pl.BlockSpec(a.shape, lambda *_: (0,) * a.ndim)

    kept = list(carried) + ([] if out is None else [out])
    specs, shapes, aliases = passing(kept, 3 + chunks + 4, 0)
    if out is None:
        shapes = shapes + [jax.ShapeDtypeStruct((total_rows, channels), jnp.bfloat16)]
    out_specs = [ANY] * (len(shapes) - 1) + [
        pl.BlockSpec((tile, channels), lambda j, t, place, *_: (place[entry_of(ids, j)] * tiles + t, 0))
    ]
    work = chunks * chunk_rows
    result = pl.pallas_call(
        functools.partial(finish_kernel, ids, block_rows, len(kept) + len(shapes) - 1),
        out_shape=shapes,
        grid_spec=pltpu.PrefetchScalarGridSpec(
            num_scalar_prefetch=3,
            grid=(chunks, tiles),
            in_specs=[chunk_spec(i) for i in range(chunks)]
            + [whole(entry_t), whole(score_t), whole(mixed), whole(final)]
            + specs,
            out_specs=out_specs,
            scratch_shapes=[pltpu.VMEM((tile, channels), jnp.bfloat16)],
        ),
        input_output_aliases=aliases,
        compiler_params=pltpu.CompilerParams(vmem_limit_bytes=48 * MIB),
        cost_estimate=HIDDEN,
        name="finish",
    )(
        place,
        valid,
        factors,
        *(pltpu.with_memory_space_constraint(x, pltpu.HBM) for x in xs),
        entry_t,
        score_t,
        mixed,
        final,
        *kept,
    )
    return result[-1], result[:-1]


def per_device(
    element_attribute_table,
    active_group_tally,
    group_destination_part,
    element_vertex_permutation,
    softness_factor,
    entry_projection_coefficients,
    partition_score_coefficients,
    summary_query_key_coefficients,
    final_projection_coefficients,
):
    block_count, block_rows = element_vertex_permutation.shape
    total_rows, channels = element_attribute_table.shape
    heads, width, slices = partition_score_coefficients.shape
    shards = lax.axis_size("pts")
    here = lax.axis_index("pts")
    per_peer = max(1, (block_count + shards - 1) // shards)
    chunk_rows = per_peer * block_rows

    inner = 1 << (shards.bit_length() // 2)
    assert shards & (shards - 1) == 0 and heads % inner == 0
    outer = shards // inner

    def send(chunk, k):
        return lax.ppermute(chunk, "pts", [(i, i ^ k) for i in range(shards)])

    far = list(range(shards // 2, shards))
    near = list(range(1, shards // 2))
    first, second = far[:1], far[1:3]
    late = [far[6 + i : 7 + i] + near[3 + 2 * i : 5 + 2 * i] for i in range(len(far) - 6)]
    third = near[:2] + far[3:5] + far[5:6] + near[2:3] + [k for wave in late for k in wave] + [0]
    ranks = first + second + third
    groups = [[0] + far[:2], far[2:3] + near[:2], far[3:4] + near[2:3]]
    groups += [far[4 + i : 5 + i] + near[3 + 2 * i : 5 + 2 * i] for i in range(len(far) - 4)]

    factors = LOG2E / softness_factor
    entry_t = entry_projection_coefficients.T
    score_t = partition_score_coefficients.transpose(0, 2, 1)
    maps_t = summary_query_key_coefficients.T

    arrived = {}
    held = {}
    at_here = here[None]
    blocks = (element_vertex_permutation, element_attribute_table)

    def gather(offsets, order):
        chunks, (order,) = gather_blocks(at_here, (slots,), *blocks, offsets, per_peer, (order,))
        held.update(zip(offsets, chunks))
        return order

    def depart(wave):
        for k in wave:
            arrived[k] = send(held.pop(k), k)

    def carry(order, *offsets):
        return (order,) + tuple(held.values()) + tuple(arrived[k] for k in offsets)

    def release(carried, wave, *offsets):
        held.update(zip(list(held), carried[1:]))
        arrived.update(zip(offsets, carried[1 + len(held) :]))
        depart(wave)
        return carried[0]

    places = (active_group_tally, group_destination_part)
    (slots, counts, *chunks), _ = gather_blocks(
        at_here, places, *blocks, first, per_peer, shards=shards
    )
    held.update(zip(first, chunks))
    depart(first)
    order = gather(second, jnp.zeros((8, 128), jnp.int32))
    depart(second[:1])

    seat = (here % inner)[None]
    rows = -(-shards * shards // slices)
    height = -(-(width + 1 + rows) // 16) * 16
    tail = jnp.where(jnp.arange(shards)[:, None] == here, counts[None, :], 0).reshape(rows, slices)
    tail = jnp.pad(tail.astype(jnp.float32), ((1, height - width - 1 - rows), (0, 0)))
    live_rows = active_group_tally * block_rows
    weights = (tail, element_attribute_table, entry_t, score_t)
    steps = 8
    nothing = jnp.zeros((8, 128))
    (begun,), carried = summarize(
        seat, live_rows, factors, nothing, *weights, (0, steps - 1, steps), 0, carry(order)
    )
    order = release(carried, second[1:2])
    pieces, carried = summarize(
        seat, live_rows, factors, begun, *weights, (steps - 1, steps, steps), inner, carry(order, far[0])
    )
    order = release(carried, [], far[0])
    parts = [pieces[0]] + [send(pieces[k], k) for k in range(1, inner)]
    piece = jax.ShapeDtypeStruct(parts[0].shape, jnp.bfloat16)
    (part,), carried = small_call(
        add_kernel, "add", parts, [piece], carry(order, far[1]), parts=inner
    )
    order = release(carried, [], far[1])
    parts = [part] + [send(part, k * inner) for k in range(1, outer)]
    order = gather(third, order)
    arrived[0] = held.pop(0)
    depart(third[:2])
    mixed = jax.ShapeDtypeStruct((heads // inner, width, slices), jnp.bfloat16)
    (mixed, tails), carried = small_call(
        attend_kernel,
        "attend",
        [maps_t] + parts,
        [mixed, jax.ShapeDtypeStruct(tail.shape, jnp.float32)],
        carry(order, far[2]),
        parts=outer,
    )
    order = release(carried, third[2:4], far[2])
    received = tails[1 : 1 + rows].reshape(shards, shards)[:, here].astype(jnp.int32)
    parts = [mixed] + [send(mixed, k) for k in range(1, inner)]
    mixed = jax.ShapeDtypeStruct((heads, width, slices), jnp.bfloat16)
    (mixed,), carried = small_call(
        join_kernel, "join", [seat] + parts, [mixed], carry(order), scalars=1, parts=inner
    )
    order = release(carried, third[4:6])

    middle_t = entry_t[channels:]
    sources = here ^ jnp.array(ranks, jnp.int32)
    out = None
    for i, group in enumerate(groups):
        out, carried = finish(
            [ranks.index(k) for k in group],
            block_rows,
            sources,
            received,
            factors,
            [arrived[k] for k in group],
            middle_t,
            score_t,
            mixed,
            final_projection_coefficients,
            out,
            shards * chunk_rows,
            carry(order),
        )
        order = release(carried, late[i] if i < len(late) else [])
    return out


def solution(mesh):
    placed = (
        P(("grp", "pts"), None),
        P(("grp", "pts")),
        P(("grp", "pts")),
        P(("grp", "pts"), None),
        P(),
        P(),
        P(),
        P(),
        P(),
    )
    return jax.shard_map(
        per_device, mesh=mesh, in_specs=placed, out_specs=P(("grp", "pts"), None), check_vma=False
    )
```

```python
import functools
import math

import jax
import jax.numpy as jnp
from jax import lax
from jax.experimental import pallas as pl
from jax.experimental.pallas import tpu as pltpu
from jax.sharding import PartitionSpec as P

NORM_EPS = 1e-05
SLICE_EPS = 1e-05
LOG2E = math.log2(math.e)
MIB = 1 << 20
EXACT = lax.Precision.HIGHEST
ANY = pl.BlockSpec(memory_space=pl.ANY)
SMEM = pl.BlockSpec(memory_space=pltpu.SMEM)
VMEM = pl.BlockSpec(memory_space=pltpu.VMEM)
HIDDEN = pl.CostEstimate(flops=0, bytes_accessed=0, transcendentals=0)


def dot(a, b, contract, precision=None):
    return lax.dot_general(
        a, b, (contract, ((), ())), preferred_element_type=jnp.float32, precision=precision
    )


def normalize_rows(point_rows):
    values = point_rows.astype(jnp.float32)
    centre = jnp.mean(values, axis=-1, keepdims=True)
    values = values - centre
    spread = jnp.mean(jnp.square(values), axis=-1, keepdims=True)
    return (values * lax.rsqrt(spread + NORM_EPS)).astype(jnp.bfloat16)


def passing(carried, first_input, first_output):
    shapes = [pltpu.HBM(a.shape, a.dtype) for a in carried]
    aliases = {first_input + i: first_output + i for i in range(len(carried))}
    return [ANY] * len(carried), shapes, aliases


def plan_slots(per_peer, tally_ref, part_ref, slots_ref, counts_ref):
    shards = counts_ref.shape[0]

    @pl.loop(0, shards)
    def _(p):
        counts_ref[p] = 0
        for q in range(per_peer):
            slots_ref[p * per_peer + q] = 0

    @pl.loop(0, tally_ref[0])
    def _(b):
        part = part_ref[b]
        at = counts_ref[part]
        slots_ref[part * per_peer + jnp.minimum(at, per_peer - 1)] = b
        counts_ref[part] = at + 1


def gather_kernel(plan, offsets, per_peer, rows, here_ref, *refs):
    count = len(offsets)
    *refs, taken, made, in_sem, out_sem = refs
    outs = refs[-count:]
    if plan:
        tally_ref, part_ref, perm_ref, table_ref, slots_ref, counts_ref = refs[:6]
        plan_slots(per_peer, tally_ref, part_ref, slots_ref, counts_ref)
    else:
        slots_ref, perm_ref, table_ref = refs[:3]

    def block(j, q):
        return slots_ref[(here_ref[0] ^ offsets[j]) * per_peer + q]

    def fetch(j, q):
        return pltpu.make_async_copy(
            table_ref.at[block(j, q)], taken.at[j, q], in_sem.at[j, q]
        )

    def store(j):
        return pltpu.make_async_copy(made.at[j], outs[j], out_sem.at[j])

    for j in range(count):

        @pl.loop(0, per_peer)
        def _(q):
            fetch(j, q).start()

    for j in range(count):

        @pl.loop(0, per_peer)
        def _(q):
            fetch(j, q).wait()
            wanted = perm_ref[pl.ds(block(j, q), 1), :]
            level = lax.broadcasted_iota(jnp.int32, (rows, rows), 0)
            picking = jnp.where(level == wanted, 1.0, 0.0).astype(jnp.bfloat16)
            made[j, pl.ds(pl.multiple_of(q * rows, rows), rows), :] = dot(
                picking, taken[j, q], ((0,), (0,))
            ).astype(jnp.bfloat16)

        store(j).start()
    for j in range(count):
        store(j).wait()


def gather_blocks(here, slots, perm, table, offsets, per_peer, carried=(), shards=0):
    count = len(offsets)
    blocks, rows = perm.shape
    channels = table.shape[-1]
    plan = len(slots) > 1
    specs, shapes, aliases = passing(carried, 3 + len(slots), 0)
    planned = [
        jax.ShapeDtypeStruct((shards * per_peer,), jnp.int32),
        jax.ShapeDtypeStruct((shards,), jnp.int32),
    ] * plan
    out = pl.pallas_call(
        functools.partial(gather_kernel, plan, offsets, per_peer, rows),
        out_shape=shapes + planned + [pltpu.HBM((per_peer * rows, channels), jnp.bfloat16)] * count,
        in_specs=[SMEM] * (1 + len(slots)) + [VMEM, ANY] + specs,
        out_specs=specs + [SMEM] * len(planned) + [ANY] * count,
        input_output_aliases=aliases,
        scratch_shapes=[
            pltpu.VMEM((count, per_peer, rows, channels), jnp.bfloat16),
            pltpu.VMEM((count, per_peer * rows, channels), jnp.bfloat16),
            pltpu.SemaphoreType.DMA((count, per_peer)),
            pltpu.SemaphoreType.DMA((count,)),
        ],
        compiler_params=pltpu.CompilerParams(vmem_limit_bytes=48 * MIB),
        cost_estimate=HIDDEN,
        name="gather_blocks",
    )(here, *slots, perm, table.reshape(blocks, rows, channels), *carried)
    return out[len(carried) :], out[: len(carried)]


def slice_powers(raw_scores, factor):
    scaled = raw_scores * factor
    return jnp.exp2(scaled - jnp.max(scaled, axis=0, keepdims=True))


def head_scores(middle, score_ref):
    heads, _, width = score_ref.shape
    made = [dot(score_ref[h], middle[h * width : (h + 1) * width], ((1,), (0,))) for h in range(1)]
    for h in range(heads):
        if h + 1 < heads:
            made.append(
                dot(score_ref[h + 1], middle[(h + 1) * width : (h + 2) * width], ((1,), (0,)))
            )
        yield h, made[h]


def summary_kernel(
    pieces, start, passed, seat_ref, live_ref, factor_ref, before_ref, tail_ref, rows_ref, entry_ref, score_ref, *refs
):
    out_refs, total = refs[passed : passed + pieces], refs[-1]
    heads, slices, width = score_ref.shape
    tile = rows_ref.shape[0]
    step = pl.program_id(0)
    channels = heads * width
    height = total.shape[1]

    @pl.when(step == 0)
    def _():
        total[...] = before_ref[...] if start else jnp.zeros_like(total)

    left = live_ref[0] - (start + step) * tile

    @pl.when(left > 0)
    def _():
        normed = normalize_rows(rows_ref[...])
        middle = dot(entry_ref[channels:, :], normed, ((1,), (1,))).astype(jnp.bfloat16)
        features = dot(entry_ref[:channels, :], normed, ((1,), (1,)))
        alive = lax.broadcasted_iota(jnp.int32, (1, tile), 1) < left
        for h, scores in head_scores(middle, score_ref):
            span = slice(h * width, (h + 1) * width)
            powers = slice_powers(scores, factor_ref[h])
            share = jnp.where(alive, 1.0 / jnp.sum(powers, axis=0, keepdims=True), 0.0)
            terms = jnp.concatenate(
                [features[span] * share, jnp.broadcast_to(share, (height - width, tile))], axis=0
            ).astype(jnp.bfloat16)
            total[h] += dot(terms, powers.astype(jnp.bfloat16), ((1,), (1,)))

    @pl.when(step == pl.num_programs(0) - 1)
    def _():
        if not pieces:
            refs[passed][...] = total[...]
        share = heads // max(pieces, 1)
        level = lax.broadcasted_iota(jnp.int32, (height - width, slices), 0)
        for p in range(pieces):
            for i in range(share):
                part = total[(seat_ref[0] ^ p) * share + i]
                rest = jnp.where(level == 0, part[width:], tail_ref[...])
                out_refs[p][i, :width] = part[:width].astype(jnp.bfloat16)
                out_refs[p][i, width:] = rest.astype(jnp.bfloat16)


def summarize(
    seat, live_rows, factors, before, tail, table, entry_t, score_t, steps, pieces, carried=()
):
    heads, slices, width = score_t.shape
    total_rows, channels = table.shape
    tile = total_rows // steps[2]
    whole = jax.ShapeDtypeStruct((heads, width + tail.shape[0], slices), jnp.float32)
    specs, shapes, aliases = passing(carried, 8, 0)
    outs = [jax.ShapeDtypeStruct((heads // max(pieces, 1),) + whole.shape[1:], jnp.bfloat16)]
    outs = outs * pieces or [whole]
    out = pl.pallas_call(
        functools.partial(summary_kernel, pieces, steps[0], 2 * len(carried)),
        grid=(steps[1] - steps[0],),
        out_shape=shapes + outs,
        in_specs=[
            SMEM,
            SMEM,
            SMEM,
            pl.BlockSpec(before.shape, lambda i: (0,) * before.ndim),
            pl.BlockSpec(tail.shape, lambda i: (0, 0)),
            pl.BlockSpec((tile, channels), lambda i: (steps[0] + i, 0)),
            pl.BlockSpec(entry_t.shape, lambda i: (0, 0)),
            pl.BlockSpec(score_t.shape, lambda i: (0, 0, 0)),
        ]
        + specs,
        out_specs=specs + [pl.BlockSpec(o.shape, lambda i: (0, 0, 0)) for o in outs],
        scratch_shapes=[pltpu.VMEM(whole.shape, jnp.float32)],
        input_output_aliases=aliases,
        compiler_params=pltpu.CompilerParams(vmem_limit_bytes=40 * MIB),
        cost_estimate=HIDDEN,
        name="summarize",
    )(
        seat,
        live_rows,
        factors,
        before,
        tail,
        pltpu.with_memory_space_constraint(table, pltpu.HBM),
        entry_t,
        score_t,
        *carried,
    )
    return out[len(carried) :], out[: len(carried)]


def small_call(kernel, name, inputs, shapes, carried, scalars=0, **kwargs):
    specs, passed, aliases = passing(carried, len(inputs), 0)
    out = pl.pallas_call(
        functools.partial(kernel, **kwargs),
        out_shape=passed + shapes,
        in_specs=[SMEM] * scalars + [VMEM] * (len(inputs) - scalars) + specs,
        out_specs=specs + [VMEM] * len(shapes),
        input_output_aliases=aliases,
        compiler_params=pltpu.CompilerParams(vmem_limit_bytes=16 * MIB),
        cost_estimate=HIDDEN,
        name=name,
    )(*inputs, *carried)
    return out[len(carried) :], out[: len(carried)]


def total_of(refs, *at):
    total = refs[0][at].astype(jnp.float32)
    for ref in refs[1:]:
        total += ref[at].astype(jnp.float32)
    return total


def add_kernel(*refs, parts):
    refs[-1][...] = total_of(refs[:parts], Ellipsis).astype(refs[-1].dtype)


def attend_kernel(*refs, parts):
    maps_ref, sums, out_ref, tail_ref = refs[0], refs[1 : 1 + parts], refs[-2], refs[-1]
    heads, width, slices = out_ref.shape
    maps = maps_ref[...].astype(jnp.float32)
    for h in range(heads):
        total = total_of(sums, h)
        tokens = total[:width] / (total[width : width + 1] + SLICE_EPS)
        project = dot(maps, tokens, ((1,), (0,)), EXACT)
        queries, keys, values = (project[i * width : (i + 1) * width] for i in range(3))
        scores = dot(keys, queries, ((0,), (0,)), EXACT) * width**-0.5
        powers = jnp.exp(scores - jnp.max(scores, axis=0, keepdims=True))
        mixed = dot(values, powers, ((1,), (0,)), EXACT)
        out_ref[h] = (mixed / jnp.sum(powers, axis=0, keepdims=True)).astype(jnp.bfloat16)
        if h == 0:
            tail_ref[...] = total[width:]


def join_kernel(seat_ref, *refs, parts):
    out_ref = refs[-1]
    share = refs[0].shape[0]
    for p in range(parts):
        out_ref[pl.ds((seat_ref[0] ^ p) * share, share)] = refs[p][...]


def entry_of(ids, chunk):
    rank = ids[0]
    for i, other in enumerate(ids[1:]):
        rank = jnp.where(chunk == i + 1, other, rank)
    return rank


def finish_kernel(ids, block_rows, extra, place_ref, valid_ref, factor_ref, *refs):
    chunks = len(ids)
    xs = refs[:chunks]
    entry_ref, score_ref, mixed_ref, final_ref = refs[chunks : chunks + 4]
    out_ref, held = refs[chunks + 4 + extra], refs[-1]
    heads, slices, width = score_ref.shape
    tile = held.shape[0]
    chunk, step = pl.program_id(0), pl.program_id(1)
    for i in range(chunks):

        @pl.when(chunk == i)
        def _():
            held[...] = xs[i][...]

    left = valid_ref[place_ref[entry_of(ids, chunk)]] * block_rows - step * tile

    @pl.when(left <= 0)
    def _():
        out_ref[...] = jnp.zeros_like(out_ref)

    @pl.when(left > 0)
    def _():
        rows = held[...]
        normed = normalize_rows(rows)
        middle = dot(entry_ref[...], normed, ((1,), (1,))).astype(jnp.bfloat16)
        spread = []
        for h, scores in head_scores(middle, score_ref):
            powers = slice_powers(scores, factor_ref[h])
            share = 1.0 / jnp.sum(powers, axis=0, keepdims=True)
            back = dot(mixed_ref[h], powers.astype(jnp.bfloat16), ((1,), (0,)))
            spread.append((back * share).astype(jnp.bfloat16))
        spread = jnp.concatenate(spread, axis=0)
        update = dot(spread, final_ref[...], ((0,), (0,)))
        done = rows.astype(jnp.float32) + update
        alive = lax.broadcasted_iota(jnp.int32, (tile, 1), 0) < left
        out_ref[...] = jnp.where(alive, done, 0.0).astype(out_ref.dtype)


def finish(
    ids, block_rows, place, valid, factors, xs, entry_t, score_t, mixed, final, out, total_rows, carried=(), tile=512
):
    heads, slices, width = score_t.shape
    chunk_rows, channels = xs[0].shape
    tile = min(tile, chunk_rows)
    tiles = chunk_rows // tile
    chunks = len(xs)

    def chunk_spec(i):
        def index(j, t, *_):
            return jnp.where(j == i, t, jnp.where(j < i, 0, tiles - 1)), 0

        return pl.BlockSpec((tile, channels), index)

    def whole(a):
        return pl.BlockSpec(a.shape, lambda *_: (0,) * a.ndim)

    kept = list(carried) + ([] if out is None else [out])
    specs, shapes, aliases = passing(kept, 3 + chunks + 4, 0)
    if out is None:
        shapes = shapes + [jax.ShapeDtypeStruct((total_rows, channels), jnp.bfloat16)]
    out_specs = [ANY] * (len(shapes) - 1) + [
        pl.BlockSpec((tile, channels), lambda j, t, place, *_: (place[entry_of(ids, j)] * tiles + t, 0))
    ]
    work = chunks * chunk_rows
    result = pl.pallas_call(
        functools.partial(finish_kernel, ids, block_rows, len(kept) + len(shapes) - 1),
        out_shape=shapes,
        grid_spec=pltpu.PrefetchScalarGridSpec(
            num_scalar_prefetch=3,
            grid=(chunks, tiles),
            in_specs=[chunk_spec(i) for i in range(chunks)]
            + [whole(entry_t), whole(score_t), whole(mixed), whole(final)]
            + specs,
            out_specs=out_specs,
            scratch_shapes=[pltpu.VMEM((tile, channels), jnp.bfloat16)],
        ),
        input_output_aliases=aliases,
        compiler_params=pltpu.CompilerParams(vmem_limit_bytes=48 * MIB),
        cost_estimate=HIDDEN,
        name="finish",
    )(
        place,
        valid,
        factors,
        *(pltpu.with_memory_space_constraint(x, pltpu.HBM) for x in xs),
        entry_t,
        score_t,
        mixed,
        final,
        *kept,
    )
    return result[-1], result[:-1]


def per_device(
    element_attribute_table,
    active_group_tally,
    group_destination_part,
    element_vertex_permutation,
    softness_factor,
    entry_projection_coefficients,
    partition_score_coefficients,
    summary_query_key_coefficients,
    final_projection_coefficients,
):
    block_count, block_rows = element_vertex_permutation.shape
    total_rows, channels = element_attribute_table.shape
    heads, width, slices = partition_score_coefficients.shape
    shards = lax.axis_size("pts")
    here = lax.axis_index("pts")
    per_peer = max(1, (block_count + shards - 1) // shards)
    chunk_rows = per_peer * block_rows

    inner = 1 << (shards.bit_length() // 2)
    assert shards & (shards - 1) == 0 and heads % inner == 0
    outer = shards // inner

    def send(chunk, k):
        return lax.ppermute(chunk, "pts", [(i, i ^ k) for i in range(shards)])

    far = list(range(shards // 2, shards))
    near = list(range(1, shards // 2))
    near = near[:2] + near[:2:-1] + near[2:3]
    first, second = far[:1], far[1:3] + near[:2]
    late = [far[6 + i : 7 + i] + near[3 + 2 * i : 5 + 2 * i] for i in range(len(far) - 6)]
    third = far[3:5] + far[5:6] + near[2:3] + [k for wave in late for k in wave] + [0]
    ranks = first + second + third
    groups = [[0] + far[:2], far[2:3] + near[:2], far[3:4] + near[2:3]]
    groups += [far[4 + i : 5 + i] + near[3 + 2 * i : 5 + 2 * i] for i in range(len(far) - 4)]

    factors = LOG2E / softness_factor
    entry_t = entry_projection_coefficients.T
    score_t = partition_score_coefficients.transpose(0, 2, 1)
    maps_t = summary_query_key_coefficients.T

    arrived = {}
    held = {}
    at_here = here[None]
    blocks = (element_vertex_permutation, element_attribute_table)

    def gather(offsets, order):
        chunks, (order,) = gather_blocks(at_here, (slots,), *blocks, offsets, per_peer, (order,))
        held.update(zip(offsets, chunks))
        return order

    def depart(wave):
        for k in wave:
            arrived[k] = send(held.pop(k), k)

    def carry(order, *offsets):
        return (order,) + tuple(held.values()) + tuple(arrived[k] for k in offsets)

    def release(carried, wave, *offsets):
        held.update(zip(list(held), carried[1:]))
        arrived.update(zip(offsets, carried[1 + len(held) :]))
        depart(wave)
        return carried[0]

    places = (active_group_tally, group_destination_part)
    (slots, counts, *chunks), _ = gather_blocks(
        at_here, places, *blocks, first, per_peer, shards=shards
    )
    held.update(zip(first, chunks))
    depart(first)
    order = gather(second, jnp.zeros((8, 128), jnp.int32))
    depart(far[1:2] + near[:2])

    seat = (here % inner)[None]
    rows = -(-shards * shards // slices)
    height = -(-(width + 1 + rows) // 16) * 16
    tail = jnp.where(jnp.arange(shards)[:, None] == here, counts[None, :], 0).reshape(rows, slices)
    tail = jnp.pad(tail.astype(jnp.float32), ((1, height - width - 1 - rows), (0, 0)))
    live_rows = active_group_tally * block_rows
    weights = (tail, element_attribute_table, entry_t, score_t)
    steps = 8
    nothing = jnp.zeros((8, 128))
    (begun,), carried = summarize(
        seat, live_rows, factors, nothing, *weights, (0, steps - 1, steps), 0, carry(order)
    )
    order = release(carried, far[2:3])
    pieces, carried = summarize(
        seat, live_rows, factors, begun, *weights, (steps - 1, steps, steps), inner, carry(order, far[0], *near[:2])
    )
    order = release(carried, [], far[0], *near[:2])
    parts = [pieces[0]] + [send(pieces[k], k) for k in range(1, inner)]
    piece = jax.ShapeDtypeStruct(parts[0].shape, jnp.bfloat16)
    (part,), carried = small_call(
        add_kernel, "add", parts, [piece], carry(order, far[1]), parts=inner
    )
    order = release(carried, [], far[1])
    parts = [part] + [send(part, k * inner) for k in range(1, outer)]
    order = gather(third, order)
    arrived[0] = held.pop(0)
    mixed = jax.ShapeDtypeStruct((heads // inner, width, slices), jnp.bfloat16)
    (mixed, tails), carried = small_call(
        attend_kernel,
        "attend",
        [maps_t] + parts,
        [mixed, jax.ShapeDtypeStruct(tail.shape, jnp.float32)],
        carry(order, far[2]),
        parts=outer,
    )
    order = release(carried, far[3:5], far[2])
    received = tails[1 : 1 + rows].reshape(shards, shards)[:, here].astype(jnp.int32)
    parts = [mixed] + [send(mixed, k) for k in range(1, inner)]
    mixed = jax.ShapeDtypeStruct((heads, width, slices), jnp.bfloat16)
    (mixed,), carried = small_call(
        join_kernel, "join", [seat] + parts, [mixed], carry(order), scalars=1, parts=inner
    )
    order = release(carried, far[5:6] + near[2:3])

    middle_t = entry_t[channels:]
    sources = here ^ jnp.array(ranks, jnp.int32)
    out = None
    for i, group in enumerate(groups):
        out, carried = finish(
            [ranks.index(k) for k in group],
            block_rows,
            sources,
            received,
            factors,
            [arrived[k] for k in group],
            middle_t,
            score_t,
            mixed,
            final_projection_coefficients,
            out,
            shards * chunk_rows,
            carry(order),
        )
        order = release(carried, late[i] if i < len(late) else [])
    return out


def solution(mesh):
    placed = (
        P(("grp", "pts"), None),
        P(("grp", "pts")),
        P(("grp", "pts")),
        P(("grp", "pts"), None),
        P(),
        P(),
        P(),
        P(),
        P(),
    )
    return jax.shard_map(
        per_device, mesh=mesh, in_specs=placed, out_specs=P(("grp", "pts"), None), check_vma=False
    )
```

```python
import functools
import math

import jax
import jax.numpy as jnp
from jax import lax
from jax.experimental import pallas as pl
from jax.experimental.pallas import tpu as pltpu
from jax.sharding import PartitionSpec as P

NORM_EPS = 1e-05
SLICE_EPS = 1e-05
LOG2E = math.log2(math.e)
MIB = 1 << 20
EXACT = lax.Precision.HIGHEST
ANY = pl.BlockSpec(memory_space=pl.ANY)
SMEM = pl.BlockSpec(memory_space=pltpu.SMEM)
VMEM = pl.BlockSpec(memory_space=pltpu.VMEM)
HIDDEN = pl.CostEstimate(flops=0, bytes_accessed=0, transcendentals=0)


def dot(a, b, contract, precision=None):
    return lax.dot_general(
        a, b, (contract, ((), ())), preferred_element_type=jnp.float32, precision=precision
    )


def normalize_rows(point_rows):
    values = point_rows.astype(jnp.float32)
    centre = jnp.mean(values, axis=-1, keepdims=True)
    values = values - centre
    spread = jnp.mean(jnp.square(values), axis=-1, keepdims=True)
    return (values * lax.rsqrt(spread + NORM_EPS)).astype(jnp.bfloat16)


def passing(carried, first_input, first_output):
    shapes = [pltpu.HBM(a.shape, a.dtype) for a in carried]
    aliases = {first_input + i: first_output + i for i in range(len(carried))}
    return [ANY] * len(carried), shapes, aliases


def plan_slots(per_peer, tally_ref, part_ref, slots_ref, counts_ref):
    shards = counts_ref.shape[0]

    @pl.loop(0, shards)
    def _(p):
        counts_ref[p] = 0
        for q in range(per_peer):
            slots_ref[p * per_peer + q] = 0

    @pl.loop(0, tally_ref[0])
    def _(b):
        part = part_ref[b]
        at = counts_ref[part]
        slots_ref[part * per_peer + jnp.minimum(at, per_peer - 1)] = b
        counts_ref[part] = at + 1


def gather_kernel(plan, offsets, per_peer, rows, here_ref, *refs):
    count = len(offsets)
    *refs, taken, made, in_sem, out_sem = refs
    outs = refs[-count:]
    if plan:
        tally_ref, part_ref, perm_ref, table_ref, slots_ref, counts_ref = refs[:6]
        plan_slots(per_peer, tally_ref, part_ref, slots_ref, counts_ref)
    else:
        slots_ref, perm_ref, table_ref = refs[:3]

    def block(j, q):
        return slots_ref[(here_ref[0] ^ offsets[j]) * per_peer + q]

    def fetch(j, q):
        return pltpu.make_async_copy(
            table_ref.at[block(j, q)], taken.at[j, q], in_sem.at[j, q]
        )

    def store(j):
        return pltpu.make_async_copy(made.at[j], outs[j], out_sem.at[j])

    for j in range(count):

        @pl.loop(0, per_peer)
        def _(q):
            fetch(j, q).start()

    for j in range(count):

        @pl.loop(0, per_peer)
        def _(q):
            fetch(j, q).wait()
            wanted = perm_ref[pl.ds(block(j, q), 1), :]
            level = lax.broadcasted_iota(jnp.int32, (rows, rows), 0)
            picking = jnp.where(level == wanted, 1.0, 0.0).astype(jnp.bfloat16)
            made[j, pl.ds(pl.multiple_of(q * rows, rows), rows), :] = dot(
                picking, taken[j, q], ((0,), (0,))
            ).astype(jnp.bfloat16)

        store(j).start()
    for j in range(count):
        store(j).wait()


def gather_blocks(here, slots, perm, table, offsets, per_peer, carried=(), shards=0):
    count = len(offsets)
    blocks, rows = perm.shape
    channels = table.shape[-1]
    plan = len(slots) > 1
    specs, shapes, aliases = passing(carried, 3 + len(slots), 0)
    planned = [
        jax.ShapeDtypeStruct((shards * per_peer,), jnp.int32),
        jax.ShapeDtypeStruct((shards,), jnp.int32),
    ] * plan
    out = pl.pallas_call(
        functools.partial(gather_kernel, plan, offsets, per_peer, rows),
        out_shape=shapes + planned + [pltpu.HBM((per_peer * rows, channels), jnp.bfloat16)] * count,
        in_specs=[SMEM] * (1 + len(slots)) + [VMEM, ANY] + specs,
        out_specs=specs + [SMEM] * len(planned) + [ANY] * count,
        input_output_aliases=aliases,
        scratch_shapes=[
            pltpu.VMEM((count, per_peer, rows, channels), jnp.bfloat16),
            pltpu.VMEM((count, per_peer * rows, channels), jnp.bfloat16),
            pltpu.SemaphoreType.DMA((count, per_peer)),
            pltpu.SemaphoreType.DMA((count,)),
        ],
        compiler_params=pltpu.CompilerParams(vmem_limit_bytes=48 * MIB),
        cost_estimate=HIDDEN,
        name="gather_blocks",
    )(here, *slots, perm, table.reshape(blocks, rows, channels), *carried)
    return out[len(carried) :], out[: len(carried)]


def slice_powers(raw_scores, factor):
    scaled = raw_scores * factor
    return jnp.exp2(scaled - jnp.max(scaled, axis=0, keepdims=True))


def head_scores(middle, score_ref):
    heads, _, width = score_ref.shape
    made = [dot(score_ref[h], middle[h * width : (h + 1) * width], ((1,), (0,))) for h in range(1)]
    for h in range(heads):
        if h + 1 < heads:
            made.append(
                dot(score_ref[h + 1], middle[(h + 1) * width : (h + 2) * width], ((1,), (0,)))
            )
        yield h, made[h]


def summary_kernel(
    pieces, start, passed, seat_ref, live_ref, factor_ref, before_ref, tail_ref, rows_ref, entry_ref, score_ref, *refs
):
    out_refs, total = refs[passed : passed + pieces], refs[-1]
    heads, slices, width = score_ref.shape
    tile = rows_ref.shape[0]
    step = pl.program_id(0)
    channels = heads * width
    height = total.shape[1]

    @pl.when(step == 0)
    def _():
        total[...] = before_ref[...] if start else jnp.zeros_like(total)

    left = live_ref[0] - (start + step) * tile

    @pl.when(left > 0)
    def _():
        normed = normalize_rows(rows_ref[...])
        middle = dot(entry_ref[channels:, :], normed, ((1,), (1,))).astype(jnp.bfloat16)
        features = dot(entry_ref[:channels, :], normed, ((1,), (1,)))
        alive = lax.broadcasted_iota(jnp.int32, (1, tile), 1) < left
        for h, scores in head_scores(middle, score_ref):
            span = slice(h * width, (h + 1) * width)
            powers = slice_powers(scores, factor_ref[h])
            share = jnp.where(alive, 1.0 / jnp.sum(powers, axis=0, keepdims=True), 0.0)
            terms = jnp.concatenate(
                [features[span] * share, jnp.broadcast_to(share, (height - width, tile))], axis=0
            ).astype(jnp.bfloat16)
            total[h] += dot(terms, powers.astype(jnp.bfloat16), ((1,), (1,)))

    @pl.when(step == pl.num_programs(0) - 1)
    def _():
        if not pieces:
            refs[passed][...] = total[...]
        share = heads // max(pieces, 1)
        level = lax.broadcasted_iota(jnp.int32, (height - width, slices), 0)
        for p in range(pieces):
            for i in range(share):
                part = total[(seat_ref[0] ^ p) * share + i]
                rest = jnp.where(level == 0, part[width:], tail_ref[...])
                out_refs[p][i, :width] = part[:width].astype(jnp.bfloat16)
                out_refs[p][i, width:] = rest.astype(jnp.bfloat16)


def summarize(
    seat, live_rows, factors, before, tail, table, entry_t, score_t, steps, pieces, carried=()
):
    heads, slices, width = score_t.shape
    total_rows, channels = table.shape
    tile = total_rows // steps[2]
    whole = jax.ShapeDtypeStruct((heads, width + tail.shape[0], slices), jnp.float32)
    specs, shapes, aliases = passing(carried, 8, 0)
    outs = [jax.ShapeDtypeStruct((heads // max(pieces, 1),) + whole.shape[1:], jnp.bfloat16)]
    outs = outs * pieces or [whole]
    out = pl.pallas_call(
        functools.partial(summary_kernel, pieces, steps[0], 2 * len(carried)),
        grid=(steps[1] - steps[0],),
        out_shape=shapes + outs,
        in_specs=[
            SMEM,
            SMEM,
            SMEM,
            pl.BlockSpec(before.shape, lambda i: (0,) * before.ndim),
            pl.BlockSpec(tail.shape, lambda i: (0, 0)),
            pl.BlockSpec((tile, channels), lambda i: (steps[0] + i, 0)),
            pl.BlockSpec(entry_t.shape, lambda i: (0, 0)),
            pl.BlockSpec(score_t.shape, lambda i: (0, 0, 0)),
        ]
        + specs,
        out_specs=specs + [pl.BlockSpec(o.shape, lambda i: (0, 0, 0)) for o in outs],
        scratch_shapes=[pltpu.VMEM(whole.shape, jnp.float32)],
        input_output_aliases=aliases,
        compiler_params=pltpu.CompilerParams(vmem_limit_bytes=40 * MIB),
        cost_estimate=HIDDEN,
        name="summarize",
    )(
        seat,
        live_rows,
        factors,
        before,
        tail,
        pltpu.with_memory_space_constraint(table, pltpu.HBM),
        entry_t,
        score_t,
        *carried,
    )
    return out[len(carried) :], out[: len(carried)]


def small_call(kernel, name, inputs, shapes, carried, scalars=0, **kwargs):
    specs, passed, aliases = passing(carried, len(inputs), 0)
    out = pl.pallas_call(
        functools.partial(kernel, **kwargs),
        out_shape=passed + shapes,
        in_specs=[SMEM] * scalars + [VMEM] * (len(inputs) - scalars) + specs,
        out_specs=specs + [VMEM] * len(shapes),
        input_output_aliases=aliases,
        compiler_params=pltpu.CompilerParams(vmem_limit_bytes=16 * MIB),
        cost_estimate=HIDDEN,
        name=name,
    )(*inputs, *carried)
    return out[len(carried) :], out[: len(carried)]


def total_of(refs, *at):
    total = refs[0][at].astype(jnp.float32)
    for ref in refs[1:]:
        total += ref[at].astype(jnp.float32)
    return total


def add_kernel(*refs, parts):
    refs[-1][...] = total_of(refs[:parts], Ellipsis).astype(refs[-1].dtype)


def attend_kernel(*refs, parts):
    maps_ref, sums, out_ref, tail_ref = refs[0], refs[1 : 1 + parts], refs[-2], refs[-1]
    heads, width, slices = out_ref.shape
    maps = maps_ref[...].astype(jnp.float32)
    for h in range(heads):
        total = total_of(sums, h)
        tokens = total[:width] / (total[width : width + 1] + SLICE_EPS)
        project = dot(maps, tokens, ((1,), (0,)), EXACT)
        queries, keys, values = (project[i * width : (i + 1) * width] for i in range(3))
        scores = dot(keys, queries, ((0,), (0,)), EXACT) * width**-0.5
        powers = jnp.exp(scores - jnp.max(scores, axis=0, keepdims=True))
        mixed = dot(values, powers, ((1,), (0,)), EXACT)
        out_ref[h] = (mixed / jnp.sum(powers, axis=0, keepdims=True)).astype(jnp.bfloat16)
        if h == 0:
            tail_ref[...] = total[width:]


def join_kernel(seat_ref, *refs, parts):
    out_ref = refs[-1]
    share = refs[0].shape[0]
    for p in range(parts):
        out_ref[pl.ds((seat_ref[0] ^ p) * share, share)] = refs[p][...]


def entry_of(ids, chunk):
    rank = ids[0]
    for i, other in enumerate(ids[1:]):
        rank = jnp.where(chunk == i + 1, other, rank)
    return rank


def finish_kernel(ids, block_rows, extra, place_ref, valid_ref, factor_ref, *refs):
    chunks = len(ids)
    xs = refs[:chunks]
    entry_ref, score_ref, mixed_ref, final_ref = refs[chunks : chunks + 4]
    out_ref, held = refs[chunks + 4 + extra], refs[-1]
    heads, slices, width = score_ref.shape
    tile = held.shape[0]
    chunk, step = pl.program_id(0), pl.program_id(1)
    for i in range(chunks):

        @pl.when(chunk == i)
        def _():
            held[...] = xs[i][...]

    left = valid_ref[place_ref[entry_of(ids, chunk)]] * block_rows - step * tile

    @pl.when(left <= 0)
    def _():
        out_ref[...] = jnp.zeros_like(out_ref)

    @pl.when(left > 0)
    def _():
        rows = held[...]
        normed = normalize_rows(rows)
        middle = dot(entry_ref[...], normed, ((1,), (1,))).astype(jnp.bfloat16)
        spread = []
        for h, scores in head_scores(middle, score_ref):
            powers = slice_powers(scores, factor_ref[h])
            share = 1.0 / jnp.sum(powers, axis=0, keepdims=True)
            back = dot(mixed_ref[h], powers.astype(jnp.bfloat16), ((1,), (0,)))
            spread.append((back * share).astype(jnp.bfloat16))
        spread = jnp.concatenate(spread, axis=0)
        update = dot(spread, final_ref[...], ((0,), (0,)))
        done = rows.astype(jnp.float32) + update
        alive = lax.broadcasted_iota(jnp.int32, (tile, 1), 0) < left
        out_ref[...] = jnp.where(alive, done, 0.0).astype(out_ref.dtype)


def finish(
    ids, block_rows, place, valid, factors, xs, entry_t, score_t, mixed, final, out, total_rows, carried=(), tile=512
):
    heads, slices, width = score_t.shape
    chunk_rows, channels = xs[0].shape
    tile = min(tile, chunk_rows)
    tiles = chunk_rows // tile
    chunks = len(xs)

    def chunk_spec(i):
        def index(j, t, *_):
            return jnp.where(j == i, t, jnp.where(j < i, 0, tiles - 1)), 0

        return pl.BlockSpec((tile, channels), index)

    def whole(a):
        return pl.BlockSpec(a.shape, lambda *_: (0,) * a.ndim)

    kept = list(carried) + ([] if out is None else [out])
    specs, shapes, aliases = passing(kept, 3 + chunks + 4, 0)
    if out is None:
        shapes = shapes + [jax.ShapeDtypeStruct((total_rows, channels), jnp.bfloat16)]
    out_specs = [ANY] * (len(shapes) - 1) + [
        pl.BlockSpec((tile, channels), lambda j, t, place, *_: (place[entry_of(ids, j)] * tiles + t, 0))
    ]
    work = chunks * chunk_rows
    result = pl.pallas_call(
        functools.partial(finish_kernel, ids, block_rows, len(kept) + len(shapes) - 1),
        out_shape=shapes,
        grid_spec=pltpu.PrefetchScalarGridSpec(
            num_scalar_prefetch=3,
            grid=(chunks, tiles),
            in_specs=[chunk_spec(i) for i in range(chunks)]
            + [whole(entry_t), whole(score_t), whole(mixed), whole(final)]
            + specs,
            out_specs=out_specs,
            scratch_shapes=[pltpu.VMEM((tile, channels), jnp.bfloat16)],
        ),
        input_output_aliases=aliases,
        compiler_params=pltpu.CompilerParams(vmem_limit_bytes=48 * MIB),
        cost_estimate=HIDDEN,
        name="finish",
    )(
        place,
        valid,
        factors,
        *(pltpu.with_memory_space_constraint(x, pltpu.HBM) for x in xs),
        entry_t,
        score_t,
        mixed,
        final,
        *kept,
    )
    return result[-1], result[:-1]


def per_device(
    element_attribute_table,
    active_group_tally,
    group_destination_part,
    element_vertex_permutation,
    softness_factor,
    entry_projection_coefficients,
    partition_score_coefficients,
    summary_query_key_coefficients,
    final_projection_coefficients,
):
    block_count, block_rows = element_vertex_permutation.shape
    total_rows, channels = element_attribute_table.shape
    heads, width, slices = partition_score_coefficients.shape
    shards = lax.axis_size("pts")
    here = lax.axis_index("pts")
    per_peer = max(1, (block_count + shards - 1) // shards)
    chunk_rows = per_peer * block_rows

    inner = 1 << (shards.bit_length() // 2)
    assert shards & (shards - 1) == 0 and heads % inner == 0
    outer = shards // inner

    def send(chunk, k):
        return lax.ppermute(chunk, "pts", [(i, i ^ k) for i in range(shards)])

    far = list(range(shards // 2, shards))
    near = list(range(1, shards // 2))
    near = near[:3] + near[:2:-1]
    first, second = far[:1], far[1:3] + near[:3]
    late = [far[6 + i : 7 + i] + near[4 + 2 * i : 6 + 2 * i] for i in range(len(far) - 6)]
    third = far[3:5] + far[5:6] + near[3:4] + [k for wave in late for k in wave] + [0]
    ranks = first + second + third
    groups = [[0] + far[:2], far[2:3] + near[:2], far[3:4] + near[2:3]]
    groups += [far[4 + i : 5 + i] + near[3 + 2 * i : 5 + 2 * i] for i in range(len(far) - 4)]

    factors = LOG2E / softness_factor
    entry_t = entry_projection_coefficients.T
    score_t = partition_score_coefficients.transpose(0, 2, 1)
    maps_t = summary_query_key_coefficients.T

    arrived = {}
    held = {}
    at_here = here[None]
    blocks = (element_vertex_permutation, element_attribute_table)

    def gather(offsets, order):
        chunks, (order,) = gather_blocks(at_here, (slots,), *blocks, offsets, per_peer, (order,))
        held.update(zip(offsets, chunks))
        return order

    def depart(wave):
        for k in wave:
            arrived[k] = send(held.pop(k), k)

    def carry(order, *offsets):
        return (order,) + tuple(held.values()) + tuple(arrived[k] for k in offsets)

    def release(carried, wave, *offsets):
        held.update(zip(list(held), carried[1:]))
        arrived.update(zip(offsets, carried[1 + len(held) :]))
        depart(wave)
        return carried[0]

    places = (active_group_tally, group_destination_part)
    (slots, counts, *chunks), _ = gather_blocks(
        at_here, places, *blocks, first, per_peer, shards=shards
    )
    held.update(zip(first, chunks))
    depart(first)
    order = gather(second, jnp.zeros((8, 128), jnp.int32))
    depart(far[1:2] + near[:3])

    seat = (here % inner)[None]
    rows = -(-shards * shards // slices)
    height = -(-(width + 1 + rows) // 16) * 16
    tail = jnp.where(jnp.arange(shards)[:, None] == here, counts[None, :], 0).reshape(rows, slices)
    tail = jnp.pad(tail.astype(jnp.float32), ((1, height - width - 1 - rows), (0, 0)))
    live_rows = active_group_tally * block_rows
    weights = (tail, element_attribute_table, entry_t, score_t)
    steps = 8
    nothing = jnp.zeros((8, 128))
    (begun,), carried = summarize(
        seat, live_rows, factors, nothing, *weights, (0, steps - 1, steps), 0, carry(order)
    )
    order = release(carried, far[2:3])
    pieces, carried = summarize(
        seat, live_rows, factors, begun, *weights, (steps - 1, steps, steps), inner, carry(order, far[0], *near[:3])
    )
    order = release(carried, [], far[0], *near[:3])
    parts = [pieces[0]] + [send(pieces[k], k) for k in range(1, inner)]
    piece = jax.ShapeDtypeStruct(parts[0].shape, jnp.bfloat16)
    (part,), carried = small_call(
        add_kernel, "add", parts, [piece], carry(order, far[1]), parts=inner
    )
    order = release(carried, [], far[1])
    parts = [part] + [send(part, k * inner) for k in range(1, outer)]
    order = gather(third, order)
    arrived[0] = held.pop(0)
    mixed = jax.ShapeDtypeStruct((heads // inner, width, slices), jnp.bfloat16)
    (mixed, tails), carried = small_call(
        attend_kernel,
        "attend",
        [maps_t] + parts,
        [mixed, jax.ShapeDtypeStruct(tail.shape, jnp.float32)],
        carry(order, far[2]),
        parts=outer,
    )
    order = release(carried, far[3:5], far[2])
    received = tails[1 : 1 + rows].reshape(shards, shards)[:, here].astype(jnp.int32)
    parts = [mixed] + [send(mixed, k) for k in range(1, inner)]
    mixed = jax.ShapeDtypeStruct((heads, width, slices), jnp.bfloat16)
    (mixed,), carried = small_call(
        join_kernel, "join", [seat] + parts, [mixed], carry(order), scalars=1, parts=inner
    )
    order = release(carried, far[5:6] + near[3:4])

    middle_t = entry_t[channels:]
    sources = here ^ jnp.array(ranks, jnp.int32)
    out = None
    for i, group in enumerate(groups):
        out, carried = finish(
            [ranks.index(k) for k in group],
            block_rows,
            sources,
            received,
            factors,
            [arrived[k] for k in group],
            middle_t,
            score_t,
            mixed,
            final_projection_coefficients,
            out,
            shards * chunk_rows,
            carry(order),
        )
        order = release(carried, late[i] if i < len(late) else [])
    return out


def solution(mesh):
    placed = (
        P(("grp", "pts"), None),
        P(("grp", "pts")),
        P(("grp", "pts")),
        P(("grp", "pts"), None),
        P(),
        P(),
        P(),
        P(),
        P(),
    )
    return jax.shard_map(
        per_device, mesh=mesh, in_specs=placed, out_specs=P(("grp", "pts"), None), check_vma=False
    )
```
